32 devices in a mesh: row: 4 (over y, x), col: 4 (over z), depth: 2 (over core).
Axes of the slice: x: 2, y: 2, z: 4, core: 2. Of those that a mesh axis runs over, the one named last changes fastest.
Arguments:
- left_store: float32 [4, 2, 16, 2, 64, 1024], P('row', 'depth', 'col'), may hold values from -6 to 6
- left_home: int32 [4, 2, 16], P('row', 'depth'), may hold values from 0 to 15, each once within a row
- up_store: float32 [4, 2, 16, 2, 64, 1024], P('col', 'depth', 'row'), may hold values from -0.3125 to 0.3125
- up_home: int32 [4, 2, 16], P('col', 'depth'), may hold values from 0 to 15, each once within a row
- targets: int32 [4, 4, 2], P('row', 'col'), may hold values from 0 to 63, as said below
- sketch: float32 [4, 4, 2, 64, 1024], P('row', 'col'), may hold values from -0.1875 to 0.1875
Outputs:
- basis: float32 [4, 4, 2, 64, 1024], P('row', 'col', 'depth')
- weights: float32 [4, 4, 2, 64, 1024], P('row', 'col', 'depth')
The draws below stay inside these ranges and needn't reach their ends.
Inputs may be any that keep to these rules, and one draw needn't show every extreme that they name: `left_home`: for each row and depth index the entries are the store positions 0 to 15, each once. `up_home`: for each col and depth index the entries are the store positions 0 to 15, each once. `targets`: the 2 entries of one row and col index are distinct.
All inputs are finite; a program needn't handle non-finite values.
Results may differ from the reference program's by a relative error of at most 0.0003.
Values sent between devices are 32-bit elements; how exact they have to be, the bound alone decides.
A program may use at most 128 MiB of HBM per device.

```python
import jax
import jax.numpy as jnp
from jax import lax

TILE = 1024
R = 64
KD = 2
RB = 8
CB = 8
TPD = 2
N_ROW = 4
N_COL = 4
N_DEPTH = 2


def draw_targets(key, part):
    keys = jax.random.split(jax.random.fold_in(key, 17), N_ROW * N_COL)
    orders = jax.vmap(lambda single: jax.random.permutation(single, RB * CB))(keys)
    return orders[:, :TPD].reshape(N_ROW, N_COL, TPD).astype(jnp.int32)


def block_scale(own_key, dims, cuts, least, top_value):
    loudness = 1.0
    for dim, blocks in cuts:
        heights = jax.random.uniform(jax.random.fold_in(jax.random.fold_in(own_key, 6), dim), (blocks,), jnp.float32, least / len(cuts), top_value / len(cuts))
        loudness = loudness * jnp.repeat(jnp.exp(heights), dims[dim] // blocks).reshape((-1,) + (1,) * (len(dims) - 1 - dim))
    return loudness


def gaussian(rng, extent, deviation, reach, cuts=(), kind=jnp.bfloat16):
    gain = block_scale(rng, extent, cuts, -0.22, 0.18) if cuts else 1.0
    drawn = jax.random.normal(rng, extent, jnp.float32) * deviation * gain
    return jnp.minimum(jnp.maximum(drawn, -reach), reach).astype(kind)


def setup_inputs(seed: int = 0) -> dict:
    key_list = jax.random.split(jax.random.key(seed), 7)
    return {
        "left_store": gaussian(key_list[0], (N_ROW, N_DEPTH, RB * KD, 2, R, TILE), 1.0, 6.0, ((0, 4), (1, 2), (2, 4)), jnp.float32),
        "left_home": jax.vmap(lambda own: jax.random.permutation(own, RB * KD))(jax.random.split(key_list[1], N_ROW * N_DEPTH)).reshape((N_ROW, N_DEPTH, RB * KD)).astype(jnp.int32),
        "up_store": gaussian(key_list[2], (N_COL, N_DEPTH, CB * KD, 2, R, TILE), (6 * R) ** -0.5, 0.3125, ((0, 4), (1, 2), (2, 4)), jnp.float32),
        "up_home": jax.vmap(lambda own: jax.random.permutation(own, CB * KD))(jax.random.split(key_list[3], N_COL * N_DEPTH)).reshape((N_COL, N_DEPTH, CB * KD)).astype(jnp.int32),
        "targets": draw_targets(jax.random.fold_in(key_list[6], 71), 0),
        "sketch": gaussian(key_list[5], (N_ROW, N_COL, TPD, R, TILE), TILE ** -0.5, 0.1875, ((0, 4), (1, 4)), jnp.float32),
    }


def orthonormal(sample):
    gram_mat = jnp.einsum('pat,pbt->pab', sample, sample, precision=lax.Precision.HIGHEST)
    factor_low = jnp.linalg.cholesky(gram_mat)
    return lax.linalg.triangular_solve(factor_low, sample, left_side=True, lower=True)

def reference(left_store, left_home, up_store, up_home, targets, sketch):
    pick = jax.vmap(jax.vmap(lambda store, home: jnp.take(store, home, axis=0)))
    left_order = pick(left_store, left_home).reshape(N_ROW, N_DEPTH, RB, KD, 2, R, TILE)
    up_order = pick(up_store, up_home).reshape(N_COL, N_DEPTH, CB, KD, 2, R, TILE)
    high = lax.Precision.HIGHEST

    def per_cell(cell):
        row_index = cell // N_COL
        col_index = cell % N_COL
        chosen = targets[row_index, col_index]
        block_row = (chosen // CB).astype(jnp.int32)
        block_col = (chosen % CB).astype(jnp.int32)
        row_pairs = jnp.take(left_order[row_index], block_row, axis=1)
        col_pairs = jnp.take(up_order[col_index], block_col, axis=1)
        row_basis = row_pairs[:, :, :, 0]
        row_coef = row_pairs[:, :, :, 1]
        col_coef = col_pairs[:, :, :, 0]
        col_basis = col_pairs[:, :, :, 1]
        test_rows = sketch[row_index, col_index]
        middle = jnp.einsum('dpkat,dpkbt->dpkab', row_coef, col_coef, precision=high)
        test_side = jnp.einsum('pat,dpkbt->dpkab', test_rows, col_basis, precision=high)
        folded = jnp.einsum('dpkab,dpkcb->dpkac', test_side, middle, precision=high)
        sampled = jnp.einsum('dpkac,dpkct->pat', folded, row_basis, precision=high)
        bases = orthonormal(sampled)
        inner_prod = jnp.einsum('pat,dpkct->dpkac', bases, row_basis, precision=high)
        turned = jnp.einsum('dpkac,dpkcb->dpkab', inner_prod, middle, precision=high)
        projected = jnp.einsum('dpkab,dpkbt->pat', turned, col_basis, precision=high)
        root_tile = jnp.sqrt(jnp.float32(TILE))
        return (bases * root_tile, projected / root_tile)
    basis, weights = lax.map(per_cell, jnp.arange(N_ROW * N_COL, dtype=jnp.int32))
    return (basis.reshape(N_ROW, N_COL, TPD, R, TILE), weights.reshape(N_ROW, N_COL, TPD, R, TILE))
```

```python
import functools
import math

import jax
import jax.numpy as jnp
from jax import lax
from jax.experimental import pallas as pl
from jax.experimental.pallas import tpu as pltpu
from jax.sharding import PartitionSpec as P

KD = 2
RB = 8
CB = 8
PIECES = 4
AHEAD = 2
HIGH = lax.Precision.HIGHEST


def mul(a, b):
    return lax.dot_general(a, b, (((1,), (0,)), ((), ())), precision=HIGH, preferred_element_type=jnp.float32)


def mul_t(a, b):
    return lax.dot_general(a, b, (((1,), (1,)), ((), ())), precision=HIGH, preferred_element_type=jnp.float32)


def inverse_factor(grams):
    n = grams[0].shape[0]
    row = lax.broadcasted_iota(jnp.int32, (n, n), 0)
    col = lax.broadcasted_iota(jnp.int32, (n, n), 1)
    eye = (row == col).astype(jnp.float32)
    work = [[jnp.concatenate([g, eye], axis=1)[i : i + 8] for i in range(0, n, 8)] for g in grams]
    sub = lax.broadcasted_iota(jnp.int32, (8, 1), 0)
    for j in range(n - 1):
        top, inside = j // 8, j % 8
        for blocks in work:
            line = blocks[top][inside : inside + 1, :]
            line = line / line[:, j : j + 1]
            for b in range(top, n // 8):
                factor = blocks[b][:, j : j + 1]
                if b == top:
                    if inside == 7:
                        continue
                    factor = jnp.where(sub > inside, factor, 0.0)
                blocks[b] = blocks[b] - factor * line
    results = []
    for blocks in work:
        whole = jnp.concatenate(blocks, axis=0)
        pivots = jnp.sum(whole[:, :n] * eye, axis=1, keepdims=True)
        results.append(whole[:, n:] / jnp.sqrt(pivots))
    return results


def ring_maps(n):
    side = math.isqrt(n)
    if side * side != n:
        return (lambda r: r), (lambda q: q)

    def swap(r):
        y, x = r // side, r % side
        return y * side + jnp.where(y % 2 == 0, x, side - 1 - x)

    return swap, swap


def kernel(sizes, tgt, lhome, uhome, left, up, sketch, out_b, out_w, *scratch):
    n_row, n_col, n_depth = sizes
    pieces = PIECES
    lbuf, scratch = scratch[:pieces], scratch[pieces:]
    ubuf, scratch = scratch[:pieces], scratch[pieces:]
    pack, scratch = scratch[:pieces], scratch[pieces:]
    (acc_m, acc_v, zpart, zrecv, hpart, hrecv, inner, linv,
     loc_sem, zs_sem, zr_sem, rs_sem, rr_sem, ks_sem, kr_sem, xs_sem, xr_sem) = scratch
    lheld, uheld = left.shape[0], up.shape[0]
    tiles, rank, width = sketch.shape
    piece = width // pieces
    slots = tiles * KD
    row, col, dep = lax.axis_index("row"), lax.axis_index("col"), lax.axis_index("depth")
    other = n_depth - 1 - dep
    to_ring, from_ring = ring_maps(n_row)
    spot = to_ring(row)
    half_way = n_row // 2

    def ring_row(offset):
        return from_ring((spot + offset + n_row) % n_row)

    right, left_of = (row, col + 1, dep), (row, col - 1, dep)
    after, before = (ring_row(1), col, dep), (ring_row(-1), col, dep)
    twin = (row, col, other)
    mesh_id = pl.DeviceIdType.MESH

    def local(t):
        cut = pl.ds(t * piece, piece)
        return (
            pltpu.make_async_copy(left.at[:, :, :, cut], lbuf[t].at[pl.ds(col * lheld, lheld)], loc_sem.at[0, t]),
            pltpu.make_async_copy(up.at[:, :, :, cut], ubuf[t].at[pl.ds(row * uheld, uheld)], loc_sem.at[1, t]),
        )

    def line_copy(way, dist, t):
        source = col - (dist - 1) if way == 0 else col + (dist - 1)
        view = lbuf[t].at[pl.ds(source * lheld, lheld)]
        return pltpu.make_async_remote_copy(
            src_ref=view, dst_ref=view, send_sem=zs_sem.at[way, dist - 1, t], recv_sem=zr_sem.at[way, dist - 1, t],
            device_id=right if way == 0 else left_of, device_id_type=mesh_id)

    def slot_copy(way, t):
        return pltpu.make_async_remote_copy(
            src_ref=pack[t].at[way], dst_ref=lbuf[t].at[pl.ds(n_col * lheld, slots)], send_sem=ks_sem.at[way, t],
            recv_sem=kr_sem.at[way, t], device_id=right if way == 0 else left_of, device_id_type=mesh_id)

    def ring_copy(way, dist, t):
        source = ring_row(1 - dist if way == 0 else dist - 1)
        view = ubuf[t].at[pl.ds(source * uheld, uheld)]
        if n_row % 2 == 0 and dist == half_way:
            view = ubuf[t].at[pl.ds(source * uheld, uheld), way]
        return pltpu.make_async_remote_copy(
            src_ref=view, dst_ref=view, send_sem=rs_sem.at[way, dist - 1, t], recv_sem=rr_sem.at[way, dist - 1, t],
            device_id=after if way == 0 else before, device_id_type=mesh_id)

    def can_send(way, dist):
        if way == 0:
            end = col < n_col - 1 if dist == 1 else col < n_col - 2
            return jnp.logical_and(col - (dist - 1) >= 0, end)
        end = col > 0 if dist == 1 else col > 1
        return jnp.logical_and(col + (dist - 1) <= n_col - 1, end)

    def receives(way, dist):
        if way == 0:
            if dist == 1:
                return col >= 1
            return jnp.logical_and(col - dist >= 0, col < n_col - 1)
        if dist == 1:
            return col <= n_col - 2
        return jnp.logical_and(col + dist <= n_col - 1, col > 0)

    far = max(n_col - 2, 1) if n_col > 1 else 0

    def left_index(c, p, k, packed):
        pos = lhome[(tgt[c, p] // CB) * KD + k]
        if not packed or n_col < 3:
            return pos
        source = pos // lheld
        by_slot = jnp.logical_or(
            jnp.logical_and(col == 0, source >= 2), jnp.logical_and(col == n_col - 1, source <= n_col - 3))
        return jnp.where(by_slot, n_col * lheld + p * KD + k, pos)

    def up_index(p, k):
        return uhome[(tgt[col, p] % CB) * KD + k]

    def send_own(t):
        for copy in local(t):
            copy.wait()
        for way in range(2):
            if n_col > 1:
                @pl.when(can_send(way, 1))
                def _():
                    line_copy(way, 1, t).start()
            if n_row > 1:
                ring_copy(way, 1, t).start()

    def fill_slots(t):
        for way in range(2):
            turn = col == n_col - 2 if way == 0 else col == 1
            goal = n_col - 1 if way == 0 else 0

            @pl.when(turn)
            def _():
                for p in range(tiles):
                    for k in range(KD):
                        pack[t][way, p * KD + k] = lbuf[t][left_index(goal, p, k, False)]
                slot_copy(way, t).start()

    def await_slots(t):
        for way in range(2):
            @pl.when(col == n_col - 1 if way == 0 else col == 0)
            def _():
                slot_copy(way, t).wait_recv()

    def accumulate(t):
        for p in range(tiles):
            tests = sketch[p, :, t * piece : (t + 1) * piece]
            for k in range(KD):
                coef = lbuf[t][left_index(col, p, k, True), 1]
                pair = ubuf[t].at[up_index(p, k)]
                middle = mul_t(coef, pair[0])
                tested = mul_t(tests, pair[1])
                if t == 0:
                    acc_m[p, k] = middle
                    acc_v[p, k] = tested
                else:
                    acc_m[p, k] += middle
                    acc_v[p, k] += tested

    for t in range(pieces):
        for copy in local(t):
            copy.start()

    barrier = pltpu.get_barrier_semaphore()
    peers = [twin] + ([after, before] if n_row > 1 else [])
    for peer in peers:
        pl.semaphore_signal(barrier, inc=1, device_id=peer, device_id_type=mesh_id)
    greeted = len(peers)
    if n_col > 1:
        for able, peer in ((col < n_col - 1, right), (col > 0, left_of)):
            @pl.when(able)
            def _():
                pl.semaphore_signal(barrier, inc=1, device_id=peer, device_id_type=mesh_id)
            greeted = greeted + able.astype(jnp.int32)
    pl.semaphore_wait(barrier, greeted)

    for t in range(min(AHEAD, pieces)):
        send_own(t)
    lag = max(n_col - 2, half_way - 1, 0)
    for step in range(pieces + lag):
        for dist in range(1, max(far, half_way) + 1):
            t = step - (dist - 1)
            if not 0 <= t < pieces:
                continue
            for way in range(2):
                if dist <= far:
                    @pl.when(receives(way, dist))
                    def _():
                        line_copy(way, dist, t).wait_recv()
                    if dist + 1 <= far:
                        @pl.when(can_send(way, dist + 1))
                        def _():
                            line_copy(way, dist + 1, t).start()
                if n_row > 1 and dist <= half_way:
                    ring_copy(way, dist, t).wait_recv()
                    if dist + 1 <= half_way:
                        ring_copy(way, dist + 1, t).start()
        if AHEAD + step < pieces:
            send_own(AHEAD + step)
        if n_col > 2:
            if 0 <= step - (n_col - 3) < pieces:
                fill_slots(step - (n_col - 3))
            if 0 <= step - (n_col - 2) < pieces:
                await_slots(step - (n_col - 2))
        if 0 <= step - lag < pieces:
            accumulate(step - lag)

    def row_basis(t, p):
        return jnp.concatenate([lbuf[t][left_index(col, p, k, True), 0] for k in range(KD)], axis=0)

    def twin_copy(which, src, dst):
        return pltpu.make_async_remote_copy(
            src_ref=src, dst_ref=dst, send_sem=xs_sem.at[which], recv_sem=xr_sem.at[which], device_id=twin, device_id_type=mesh_id)

    z_copies = [twin_copy(p, zpart.at[p], zrecv.at[p]) for p in range(tiles)]
    for p in range(tiles):
        folded = jnp.concatenate([mul_t(acc_v[p, k], acc_m[p, k]) for k in range(KD)], axis=1)
        for t in range(pieces):
            zpart[p, :, t * piece : (t + 1) * piece] = mul(folded, row_basis(t, p))
        z_copies[p].start()
    grams, sides = [], []
    for p in range(tiles):
        z_copies[p].wait()
        zpart[p] = zpart[p] + zrecv[p]
        gram, side = None, None
        for t in range(pieces):
            z = zpart[p, :, t * piece : (t + 1) * piece]
            g, s = mul_t(z, z), mul_t(z, row_basis(t, p))
            gram, side = (g, s) if t == 0 else (gram + g, side + s)
        grams.append(gram)
        sides.append(side)
    inverses = inverse_factor(grams)
    for p in range(tiles):
        linv[p] = inverses[p]
        turned = mul(inverses[p], sides[p])
        inner[p] = jnp.concatenate(
            [mul(turned[:, k * rank : (k + 1) * rank], acc_m[p, k]) for k in range(KD)], axis=1)

    owned = tiles // n_depth
    root = math.sqrt(width)

    def project(p, t):
        cols = jnp.concatenate([ubuf[t][up_index(p, k), 1] for k in range(KD)], axis=0)
        return mul(inner[p], cols)

    h_copy = twin_copy(tiles, hpart, hrecv)
    for i in range(owned):
        for t in range(pieces):
            hpart[i, :, t * piece : (t + 1) * piece] = project(other * owned + i, t)
    h_copy.start()
    for i in range(owned):
        p = dep * owned + i
        for t in range(pieces):
            cut = slice(t * piece, (t + 1) * piece)
            out_b[i, :, cut] = mul(linv[p], zpart[p, :, cut]) * root
            out_w[i, :, cut] = project(p, t)
    h_copy.wait()
    for i in range(owned):
        out_w[i] = (out_w[i] + hrecv[i]) / root

    for t in range(pieces):
        for way in range(2):
            for dist in range(1, far + 1):
                @pl.when(can_send(way, dist))
                def _():
                    line_copy(way, dist, t).wait_send()
            if n_col > 2:
                @pl.when(col == n_col - 2 if way == 0 else col == 1)
                def _():
                    slot_copy(way, t).wait_send()
            if n_row > 1:
                for dist in range(1, half_way + 1):
                    ring_copy(way, dist, t).wait_send()


def solution(mesh):
    sizes = tuple(mesh.shape[a] for a in ("row", "col", "depth"))
    n_row, n_col, n_depth = sizes

    def shards(left_store, left_home, up_store, up_home, targets, sketch):
        lheld, _, rank, width = left_store.shape[2:]
        uheld = up_store.shape[2]
        tiles = targets.shape[2]
        slots = tiles * KD
        owned = tiles // n_depth
        piece = width // PIECES
        all_targets = lax.all_gather(targets[0], "col", axis=0, tiled=True)
        f32 = jnp.float32
        dma = pltpu.SemaphoreType.DMA
        far, half_way = max(n_col - 2, 1), max(n_row // 2, 1)
        out = jax.ShapeDtypeStruct((owned, rank, width), f32)
        vmem, smem = pl.BlockSpec(memory_space=pltpu.VMEM), pl.BlockSpec(memory_space=pltpu.SMEM)
        anywhere = pl.BlockSpec(memory_space=pl.ANY)
        basis, weights = pl.pallas_call(
            functools.partial(kernel, sizes),
            out_shape=(out, out),
            in_specs=[smem, smem, smem, anywhere, anywhere, vmem],
            out_specs=(vmem, vmem),
            scratch_shapes=[pltpu.VMEM((n_col * lheld + slots, 2, rank, piece), f32)] * PIECES
            + [pltpu.VMEM((n_row * uheld, 2, rank, piece), f32)] * PIECES
            + [pltpu.VMEM((2, slots, 2, rank, piece), f32)] * PIECES
            + [
                pltpu.VMEM((tiles, KD, rank, rank), f32),
                pltpu.VMEM((tiles, KD, rank, rank), f32),
                pltpu.VMEM((tiles, rank, width), f32),
                pltpu.VMEM((tiles, rank, width), f32),
                pltpu.VMEM((owned, rank, width), f32),
                pltpu.VMEM((owned, rank, width), f32),
                pltpu.VMEM((tiles, rank, KD * rank), f32),
                pltpu.VMEM((tiles, rank, rank), f32),
                dma((2, PIECES)),
                dma((2, far, PIECES)),
                dma((2, far, PIECES)),
                dma((2, half_way, PIECES)),
                dma((2, half_way, PIECES)),
                dma((2, PIECES)),
                dma((2, PIECES)),
                dma((tiles + 1,)),
                dma((tiles + 1,)),
            ],
            compiler_params=pltpu.CompilerParams(
                collective_id=0, has_side_effects=True, vmem_limit_bytes=48 * 1024 * 1024),
        )(all_targets, left_home[0, 0], up_home[0, 0], left_store[0, 0], up_store[0, 0], sketch[0, 0])
        return basis[None, None], weights[None, None]

    return jax.shard_map(
        shards,
        mesh=mesh,
        in_specs=(
            P("row", "depth", "col", None, None, None),
            P("row", "depth", None),
            P("col", "depth", "row", None, None, None),
            P("col", "depth", None),
            P("row", "col", None),
            P("row", "col", None, None, None),
        ),
        out_specs=(P("row", "col", "depth", None, None), P("row", "col", "depth", None, None)),
        check_vma=False,
    )
```

```python
import functools
import math

import jax
import jax.numpy as jnp
from jax import lax
from jax.experimental import pallas as pl
from jax.experimental.pallas import tpu as pltpu
from jax.sharding import PartitionSpec as P

KD = 2
RB = 8
CB = 8
PIECES = 4
AHEAD = 2
HIGH = lax.Precision.HIGHEST


def mul(a, b):
    return lax.dot_general(a, b, (((1,), (0,)), ((), ())), precision=HIGH, preferred_element_type=jnp.float32)


def mul_t(a, b):
    return lax.dot_general(a, b, (((1,), (1,)), ((), ())), precision=HIGH, preferred_element_type=jnp.float32)


def inverse_factor(grams):
    n = grams[0].shape[0]
    row = lax.broadcasted_iota(jnp.int32, (n, n), 0)
    col = lax.broadcasted_iota(jnp.int32, (n, n), 1)
    eye = (row == col).astype(jnp.float32)
    work = [[jnp.concatenate([g, eye], axis=1)[i : i + 8] for i in range(0, n, 8)] for g in grams]
    sub = lax.broadcasted_iota(jnp.int32, (8, 1), 0)
    for j in range(n - 1):
        top, inside = j // 8, j % 8
        for blocks in work:
            line = blocks[top][inside : inside + 1, :]
            line = line / line[:, j : j + 1]
            for b in range(top, n // 8):
                factor = blocks[b][:, j : j + 1]
                if b == top:
                    if inside == 7:
                        continue
                    factor = jnp.where(sub > inside, factor, 0.0)
                blocks[b] = blocks[b] - factor * line
    results = []
    for blocks in work:
        whole = jnp.concatenate(blocks, axis=0)
        pivots = jnp.sum(whole[:, :n] * eye, axis=1, keepdims=True)
        results.append(whole[:, n:] / jnp.sqrt(pivots))
    return results


def ring_maps(n):
    side = math.isqrt(n)
    if side * side != n:
        return (lambda r: r), (lambda q: q)

    def swap(r):
        y, x = r // side, r % side
        return y * side + jnp.where(y % 2 == 0, x, side - 1 - x)

    return swap, swap


def kernel(sizes, tgt_in, lhome_in, uhome_in, left_in, up_in, sketch_in, out_b, out_w, *scratch):
    n_row, n_col, n_depth = sizes
    pieces = PIECES
    lbuf, scratch = scratch[:pieces], scratch[pieces:]
    ubuf, scratch = scratch[:pieces], scratch[pieces:]
    pack, scratch = scratch[:pieces], scratch[pieces:]
    (acc_m, acc_v, zpart, zrecv, hpart, hrecv, inner, linv,
     tgt, tgt_end, lhome, uhome, sketch, tab_sem, ts_sem, tr_sem, loc_sem, zs_sem, zr_sem, rs_sem, rr_sem, ks_sem, kr_sem, xs_sem, xr_sem) = scratch
    left, up = left_in.at[0, 0], up_in.at[0, 0]
    lheld, uheld = left.shape[0], up.shape[0]
    tiles, rank, width = sketch.shape
    piece = width // pieces
    slots = tiles * KD
    row, col, dep = lax.axis_index("row"), lax.axis_index("col"), lax.axis_index("depth")
    other = n_depth - 1 - dep
    to_ring, from_ring = ring_maps(n_row)
    spot = to_ring(row)
    half_way = n_row // 2

    def ring_row(offset):
        return from_ring((spot + offset + n_row) % n_row)

    right, left_of = (row, col + 1, dep), (row, col - 1, dep)
    after, before = (ring_row(1), col, dep), (ring_row(-1), col, dep)
    twin = (row, col, other)
    mesh_id = pl.DeviceIdType.MESH

    def local(t):
        cut = pl.ds(t * piece, piece)
        return (
            pltpu.make_async_copy(left.at[:, :, :, cut], lbuf[t].at[pl.ds(col * lheld, lheld)], loc_sem.at[0, t]),
            pltpu.make_async_copy(up.at[:, :, :, cut], ubuf[t].at[pl.ds(row * uheld, uheld)], loc_sem.at[1, t]),
        )

    def line_copy(way, dist, t):
        source = col - (dist - 1) if way == 0 else col + (dist - 1)
        view = lbuf[t].at[pl.ds(source * lheld, lheld)]
        return pltpu.make_async_remote_copy(
            src_ref=view, dst_ref=view, send_sem=zs_sem.at[way, dist - 1, t], recv_sem=zr_sem.at[way, dist - 1, t],
            device_id=right if way == 0 else left_of, device_id_type=mesh_id)

    def slot_copy(way, t):
        return pltpu.make_async_remote_copy(
            src_ref=pack[t].at[way], dst_ref=lbuf[t].at[pl.ds(n_col * lheld, slots)], send_sem=ks_sem.at[way, t],
            recv_sem=kr_sem.at[way, t], device_id=right if way == 0 else left_of, device_id_type=mesh_id)

    def ring_copy(way, dist, t):
        source = ring_row(1 - dist if way == 0 else dist - 1)
        view = ubuf[t].at[pl.ds(source * uheld, uheld)]
        if n_row % 2 == 0 and dist == half_way:
            view = ubuf[t].at[pl.ds(source * uheld, uheld), way]
        return pltpu.make_async_remote_copy(
            src_ref=view, dst_ref=view, send_sem=rs_sem.at[way, dist - 1, t], recv_sem=rr_sem.at[way, dist - 1, t],
            device_id=after if way == 0 else before, device_id_type=mesh_id)

    def can_send(way, dist):
        if way == 0:
            end = col < n_col - 1 if dist == 1 else col < n_col - 2
            return jnp.logical_and(col - (dist - 1) >= 0, end)
        end = col > 0 if dist == 1 else col > 1
        return jnp.logical_and(col + (dist - 1) <= n_col - 1, end)

    def receives(way, dist):
        if way == 0:
            if dist == 1:
                return col >= 1
            return jnp.logical_and(col - dist >= 0, col < n_col - 1)
        if dist == 1:
            return col <= n_col - 2
        return jnp.logical_and(col + dist <= n_col - 1, col > 0)

    far = max(n_col - 2, 1) if n_col > 1 else 0

    def left_index(table, p, k, packed):
        pos = lhome[0, 0, (table[0, 0, p] // CB) * KD + k]
        if not packed or n_col < 3:
            return pos
        source = pos // lheld
        by_slot = jnp.logical_or(
            jnp.logical_and(col == 0, source >= 2), jnp.logical_and(col == n_col - 1, source <= n_col - 3))
        return jnp.where(by_slot, n_col * lheld + p * KD + k, pos)

    def up_index(p, k):
        return uhome[0, 0, (tgt[0, 0, p] % CB) * KD + k]

    def send_own(t):
        for copy in local(t):
            copy.wait()
        for way in range(2):
            if n_col > 1:
                @pl.when(can_send(way, 1))
                def _():
                    line_copy(way, 1, t).start()
            if n_row > 1:
                ring_copy(way, 1, t).start()

    def fill_slots(t):
        for way in range(2):
            turn = col == n_col - 2 if way == 0 else col == 1

            @pl.when(turn)
            def _():
                if t == 0:
                    target_copy(way).wait_recv()
                for p in range(tiles):
                    for k in range(KD):
                        pack[t][way, p * KD + k] = lbuf[t][left_index(tgt_end.at[way], p, k, False)]
                slot_copy(way, t).start()

    def await_slots(t):
        for way in range(2):
            @pl.when(col == n_col - 1 if way == 0 else col == 0)
            def _():
                slot_copy(way, t).wait_recv()

    def accumulate(t):
        for p in range(tiles):
            tests = sketch[p, :, t * piece : (t + 1) * piece]
            for k in range(KD):
                coef = lbuf[t][left_index(tgt, p, k, True), 1]
                pair = ubuf[t].at[up_index(p, k)]
                middle = mul_t(coef, pair[0])
                tested = mul_t(tests, pair[1])
                if t == 0:
                    acc_m[p, k] = middle
                    acc_v[p, k] = tested
                else:
                    acc_m[p, k] += middle
                    acc_v[p, k] += tested

    tables = [
        pltpu.make_async_copy(src, dst, tab_sem.at[i])
        for i, (src, dst) in enumerate(((tgt_in, tgt), (lhome_in, lhome), (uhome_in, uhome), (sketch_in.at[0, 0], sketch)))
    ]

    def target_copy(way):
        return pltpu.make_async_remote_copy(
            src_ref=tgt_in, dst_ref=tgt_end.at[way], send_sem=ts_sem.at[way], recv_sem=tr_sem.at[way],
            device_id=left_of if way == 0 else right, device_id_type=mesh_id)

    for t in range(pieces):
        for copy in local(t):
            copy.start()
    for copy in tables:
        copy.start()

    barrier = pltpu.get_barrier_semaphore()
    peers = [twin] + ([after, before] if n_row > 1 else [])
    for peer in peers:
        pl.semaphore_signal(barrier, inc=1, device_id=peer, device_id_type=mesh_id)
    greeted = len(peers)
    if n_col > 1:
        for able, peer in ((col < n_col - 1, right), (col > 0, left_of)):
            @pl.when(able)
            def _():
                pl.semaphore_signal(barrier, inc=1, device_id=peer, device_id_type=mesh_id)
            greeted = greeted + able.astype(jnp.int32)
    pl.semaphore_wait(barrier, greeted)

    if n_col > 2:
        for way in range(2):
            @pl.when(col == n_col - 1 if way == 0 else col == 0)
            def _():
                target_copy(way).start()
    for t in range(min(AHEAD, pieces)):
        send_own(t)
    for copy in tables:
        copy.wait()
    lag = max(n_col - 2, half_way - 1, 0)
    for step in range(pieces + lag):
        for dist in range(1, max(far, half_way) + 1):
            t = step - (dist - 1)
            if not 0 <= t < pieces:
                continue
            for way in range(2):
                if dist <= far:
                    @pl.when(receives(way, dist))
                    def _():
                        line_copy(way, dist, t).wait_recv()
                    if dist + 1 <= far:
                        @pl.when(can_send(way, dist + 1))
                        def _():
                            line_copy(way, dist + 1, t).start()
                if n_row > 1 and dist <= half_way:
                    ring_copy(way, dist, t).wait_recv()
                    if dist + 1 <= half_way:
                        ring_copy(way, dist + 1, t).start()
        if AHEAD + step < pieces:
            send_own(AHEAD + step)
        if n_col > 2:
            if 0 <= step - (n_col - 3) < pieces:
                fill_slots(step - (n_col - 3))
            if 0 <= step - (n_col - 2) < pieces:
                await_slots(step - (n_col - 2))
        if 0 <= step - lag < pieces:
            accumulate(step - lag)

    def row_basis(t, p):
        return jnp.concatenate([lbuf[t][left_index(tgt, p, k, True), 0] for k in range(KD)], axis=0)

    def twin_copy(which, src, dst):
        return pltpu.make_async_remote_copy(
            src_ref=src, dst_ref=dst, send_sem=xs_sem.at[which], recv_sem=xr_sem.at[which], device_id=twin, device_id_type=mesh_id)

    z_copies = [twin_copy(p, zpart.at[p], zrecv.at[p]) for p in range(tiles)]
    for p in range(tiles):
        folded = jnp.concatenate([mul_t(acc_v[p, k], acc_m[p, k]) for k in range(KD)], axis=1)
        for t in range(pieces):
            zpart[p, :, t * piece : (t + 1) * piece] = mul(folded, row_basis(t, p))
        z_copies[p].start()
    grams, sides = [], []
    for p in range(tiles):
        z_copies[p].wait()
        zpart[p] = zpart[p] + zrecv[p]
        gram, side = None, None
        for t in range(pieces):
            z = zpart[p, :, t * piece : (t + 1) * piece]
            g, s = mul_t(z, z), mul_t(z, row_basis(t, p))
            gram, side = (g, s) if t == 0 else (gram + g, side + s)
        grams.append(gram)
        sides.append(side)
    inverses = inverse_factor(grams)
    for p in range(tiles):
        linv[p] = inverses[p]
        turned = mul(inverses[p], sides[p])
        inner[p] = jnp.concatenate(
            [mul(turned[:, k * rank : (k + 1) * rank], acc_m[p, k]) for k in range(KD)], axis=1)

    owned = tiles // n_depth
    root = math.sqrt(width)

    def project(p, t):
        cols = jnp.concatenate([ubuf[t][up_index(p, k), 1] for k in range(KD)], axis=0)
        return mul(inner[p], cols)

    h_copy = twin_copy(tiles, hpart, hrecv)
    for i in range(owned):
        for t in range(pieces):
            hpart[i, :, t * piece : (t + 1) * piece] = project(other * owned + i, t)
    h_copy.start()
    for i in range(owned):
        p = dep * owned + i
        for t in range(pieces):
            cut = slice(t * piece, (t + 1) * piece)
            out_b[i, :, cut] = mul(linv[p], zpart[p, :, cut]) * root
            out_w[i, :, cut] = project(p, t)
    h_copy.wait()
    for i in range(owned):
        out_w[i] = (out_w[i] + hrecv[i]) / root

    if n_col > 2:
        for way in range(2):
            @pl.when(col == n_col - 1 if way == 0 else col == 0)
            def _():
                target_copy(way).wait_send()
    for t in range(pieces):
        for way in range(2):
            for dist in range(1, far + 1):
                @pl.when(can_send(way, dist))
                def _():
                    line_copy(way, dist, t).wait_send()
            if n_col > 2:
                @pl.when(col == n_col - 2 if way == 0 else col == 1)
                def _():
                    slot_copy(way, t).wait_send()
            if n_row > 1:
                for dist in range(1, half_way + 1):
                    ring_copy(way, dist, t).wait_send()


def solution(mesh):
    sizes = tuple(mesh.shape[a] for a in ("row", "col", "depth"))
    n_row, n_col, n_depth = sizes

    def shards(left_store, left_home, up_store, up_home, targets, sketch):
        lheld, _, rank, width = left_store.shape[2:]
        uheld = up_store.shape[2]
        tiles = targets.shape[2]
        slots = tiles * KD
        owned = tiles // n_depth
        piece = width // PIECES
        f32 = jnp.float32
        dma = pltpu.SemaphoreType.DMA
        far, half_way = max(n_col - 2, 1), max(n_row // 2, 1)
        out = jax.ShapeDtypeStruct((owned, rank, width), f32)
        vmem, smem = pl.BlockSpec(memory_space=pltpu.VMEM), pltpu.SMEM
        anywhere = pl.BlockSpec(memory_space=pl.ANY)
        basis, weights = pl.pallas_call(
            functools.partial(kernel, sizes),
            out_shape=(out, out),
            in_specs=[anywhere] * 6,
            out_specs=(vmem, vmem),
            scratch_shapes=[pltpu.VMEM((n_col * lheld + slots, 2, rank, piece), f32)] * PIECES
            + [pltpu.VMEM((n_row * uheld, 2, rank, piece), f32)] * PIECES
            + [pltpu.VMEM((2, slots, 2, rank, piece), f32)] * PIECES
            + [
                pltpu.VMEM((tiles, KD, rank, rank), f32),
                pltpu.VMEM((tiles, KD, rank, rank), f32),
                pltpu.VMEM((tiles, rank, width), f32),
                pltpu.VMEM((tiles, rank, width), f32),
                pltpu.VMEM((owned, rank, width), f32),
                pltpu.VMEM((owned, rank, width), f32),
                pltpu.VMEM((tiles, rank, KD * rank), f32),
                pltpu.VMEM((tiles, rank, rank), f32),
                smem(targets.shape, jnp.int32),
                smem((2,) + targets.shape, jnp.int32),
                smem(left_home.shape, jnp.int32),
                smem(up_home.shape, jnp.int32),
                pltpu.VMEM(sketch.shape[2:], f32),
                dma((4,)),
                dma((2,)),
                dma((2,)),
                dma((2, PIECES)),
                dma((2, far, PIECES)),
                dma((2, far, PIECES)),
                dma((2, half_way, PIECES)),
                dma((2, half_way, PIECES)),
                dma((2, PIECES)),
                dma((2, PIECES)),
                dma((tiles + 1,)),
                dma((tiles + 1,)),
            ],
            compiler_params=pltpu.CompilerParams(
                collective_id=0, has_side_effects=True, vmem_limit_bytes=60 * 1024 * 1024),
        )(targets, left_home, up_home, left_store, up_store, sketch)
        return basis[None, None], weights[None, None]

    return jax.shard_map(
        shards,
        mesh=mesh,
        in_specs=(
            P("row", "depth", "col", None, None, None),
            P("row", "depth", None),
            P("col", "depth", "row", None, None, None),
            P("col", "depth", None),
            P("row", "col", None),
            P("row", "col", None, None, None),
        ),
        out_specs=(P("row", "col", "depth", None, None), P("row", "col", "depth", None, None)),
        check_vma=False,
    )
```

```python
import functools
import math

import jax
import jax.numpy as jnp
from jax import lax
from jax.experimental import pallas as pl
from jax.experimental.pallas import tpu as pltpu
from jax.sharding import PartitionSpec as P

KD = 2
RB = 8
CB = 8
PIECES = 8
AHEAD = 3
HIGH = lax.Precision.HIGHEST


def mul(a, b):
    return lax.dot_general(a, b, (((1,), (0,)), ((), ())), precision=HIGH, preferred_element_type=jnp.float32)


def mul_t(a, b):
    return lax.dot_general(a, b, (((1,), (1,)), ((), ())), precision=HIGH, preferred_element_type=jnp.float32)


def inverse_factor(grams):
    n = grams[0].shape[0]
    row = lax.broadcasted_iota(jnp.int32, (n, n), 0)
    col = lax.broadcasted_iota(jnp.int32, (n, n), 1)
    eye = (row == col).astype(jnp.float32)
    work = [[jnp.concatenate([g, eye], axis=1)[i : i + 8] for i in range(0, n, 8)] for g in grams]
    sub = lax.broadcasted_iota(jnp.int32, (8, 1), 0)
    for j in range(n - 1):
        top, inside = j // 8, j % 8
        for blocks in work:
            line = blocks[top][inside : inside + 1, :]
            line = line / line[:, j : j + 1]
            for b in range(top, n // 8):
                factor = blocks[b][:, j : j + 1]
                if b == top:
                    if inside == 7:
                        continue
                    factor = jnp.where(sub > inside, factor, 0.0)
                blocks[b] = blocks[b] - factor * line
    results = []
    for blocks in work:
        whole = jnp.concatenate(blocks, axis=0)
        pivots = jnp.sum(whole[:, :n] * eye, axis=1, keepdims=True)
        results.append(whole[:, n:] / jnp.sqrt(pivots))
    return results


def ring_maps(n):
    side = math.isqrt(n)
    if side * side != n:
        return (lambda r: r), (lambda q: q)

    def swap(r):
        y, x = r // side, r % side
        return y * side + jnp.where(y % 2 == 0, x, side - 1 - x)

    return swap, swap


def kernel(sizes, tgt_in, lhome_in, uhome_in, left_in, up_in, sketch_in, out_b, out_w, *scratch):
    n_row, n_col, n_depth = sizes
    pieces = PIECES
    lbuf, scratch = scratch[:pieces], scratch[pieces:]
    ubuf, scratch = scratch[:pieces], scratch[pieces:]
    pack, scratch = scratch[:pieces], scratch[pieces:]
    (acc_m, acc_v, zpart, zrecv, hpart, hrecv, inner, linv,
     tgt, tgt_end, lhome, uhome, sketch, tab_sem, ts_sem, tr_sem, loc_sem, zs_sem, zr_sem, rs_sem, rr_sem, ks_sem, kr_sem, xs_sem, xr_sem) = scratch
    left, up = left_in.at[0, 0], up_in.at[0, 0]
    lheld, uheld = left.shape[0], up.shape[0]
    tiles, rank, width = sketch.shape
    piece = width // pieces
    slots = tiles * KD
    row, col, dep = lax.axis_index("row"), lax.axis_index("col"), lax.axis_index("depth")
    other = n_depth - 1 - dep
    to_ring, from_ring = ring_maps(n_row)
    spot = to_ring(row)
    half_way = n_row // 2

    def ring_row(offset):
        return from_ring((spot + offset + n_row) % n_row)

    right, left_of = (row, col + 1, dep), (row, col - 1, dep)
    after, before = (ring_row(1), col, dep), (ring_row(-1), col, dep)
    twin = (row, col, other)
    mesh_id = pl.DeviceIdType.MESH

    def local(t):
        cut = pl.ds(t * piece, piece)
        return (
            pltpu.make_async_copy(left.at[:, :, :, cut], lbuf[t].at[pl.ds(col * lheld, lheld)], loc_sem.at[0, t]),
            pltpu.make_async_copy(up.at[:, :, :, cut], ubuf[t].at[pl.ds(row * uheld, uheld)], loc_sem.at[1, t]),
        )

    def line_copy(way, dist, t):
        source = col - (dist - 1) if way == 0 else col + (dist - 1)
        view = lbuf[t].at[pl.ds(source * lheld, lheld)]
        return pltpu.make_async_remote_copy(
            src_ref=view, dst_ref=view, send_sem=zs_sem.at[way, dist - 1, t], recv_sem=zr_sem.at[way, dist - 1, t],
            device_id=right if way == 0 else left_of, device_id_type=mesh_id)

    def slot_copy(way, t):
        return pltpu.make_async_remote_copy(
            src_ref=pack[t].at[way], dst_ref=lbuf[t].at[pl.ds(n_col * lheld, slots)], send_sem=ks_sem.at[way, t],
            recv_sem=kr_sem.at[way, t], device_id=right if way == 0 else left_of, device_id_type=mesh_id)

    def ring_copy(way, dist, t):
        source = ring_row(1 - dist if way == 0 else dist - 1)
        view = ubuf[t].at[pl.ds(source * uheld, uheld)]
        if n_row % 2 == 0 and dist == half_way:
            view = ubuf[t].at[pl.ds(source * uheld, uheld), way]
        return pltpu.make_async_remote_copy(
            src_ref=view, dst_ref=view, send_sem=rs_sem.at[way, dist - 1, t], recv_sem=rr_sem.at[way, dist - 1, t],
            device_id=after if way == 0 else before, device_id_type=mesh_id)

    def can_send(way, dist):
        if way == 0:
            end = col < n_col - 1 if dist == 1 else col < n_col - 2
            return jnp.logical_and(col - (dist - 1) >= 0, end)
        end = col > 0 if dist == 1 else col > 1
        return jnp.logical_and(col + (dist - 1) <= n_col - 1, end)

    def receives(way, dist):
        if way == 0:
            if dist == 1:
                return col >= 1
            return jnp.logical_and(col - dist >= 0, col < n_col - 1)
        if dist == 1:
            return col <= n_col - 2
        return jnp.logical_and(col + dist <= n_col - 1, col > 0)

    far = max(n_col - 2, 1) if n_col > 1 else 0

    def left_index(table, p, k, packed):
        pos = lhome[0, 0, (table[0, 0, p] // CB) * KD + k]
        if not packed or n_col < 3:
            return pos
        source = pos // lheld
        by_slot = jnp.logical_or(
            jnp.logical_and(col == 0, source >= 2), jnp.logical_and(col == n_col - 1, source <= n_col - 3))
        return jnp.where(by_slot, n_col * lheld + p * KD + k, pos)

    def up_index(p, k):
        return uhome[0, 0, (tgt[0, 0, p] % CB) * KD + k]

    def send_own(t):
        for copy in local(t):
            copy.wait()
        for way in range(2):
            if n_col > 1:
                @pl.when(can_send(way, 1))
                def _():
                    line_copy(way, 1, t).start()
            if n_row > 1:
                ring_copy(way, 1, t).start()

    def fill_slots(t):
        for way in range(2):
            turn = col == n_col - 2 if way == 0 else col == 1

            @pl.when(turn)
            def _():
                if t == 0:
                    target_copy(way).wait_recv()
                for p in range(tiles):
                    for k in range(KD):
                        pack[t][way, p * KD + k] = lbuf[t][left_index(tgt_end.at[way], p, k, False)]
                slot_copy(way, t).start()

    def await_slots(t):
        for way in range(2):
            @pl.when(col == n_col - 1 if way == 0 else col == 0)
            def _():
                slot_copy(way, t).wait_recv()

    def accumulate(t):
        for p in range(tiles):
            tests = sketch[p, :, t * piece : (t + 1) * piece]
            for k in range(KD):
                coef = lbuf[t][left_index(tgt, p, k, True), 1]
                pair = ubuf[t].at[up_index(p, k)]
                middle = mul_t(coef, pair[0])
                tested = mul_t(tests, pair[1])
                if t == 0:
                    acc_m[p, k] = middle
                    acc_v[p, k] = tested
                else:
                    acc_m[p, k] += middle
                    acc_v[p, k] += tested

    tables = [
        pltpu.make_async_copy(src, dst, tab_sem.at[i])
        for i, (src, dst) in enumerate(((tgt_in, tgt), (lhome_in, lhome), (uhome_in, uhome), (sketch_in.at[0, 0], sketch)))
    ]

    def target_copy(way):
        return pltpu.make_async_remote_copy(
            src_ref=tgt_in, dst_ref=tgt_end.at[way], send_sem=ts_sem.at[way], recv_sem=tr_sem.at[way],
            device_id=left_of if way == 0 else right, device_id_type=mesh_id)

    for t in range(pieces):
        for copy in local(t):
            copy.start()
    for copy in tables:
        copy.start()

    barrier = pltpu.get_barrier_semaphore()
    peers = [twin] + ([after, before] if n_row > 1 else [])
    for peer in peers:
        pl.semaphore_signal(barrier, inc=1, device_id=peer, device_id_type=mesh_id)
    greeted = len(peers)
    if n_col > 1:
        for able, peer in ((col < n_col - 1, right), (col > 0, left_of)):
            @pl.when(able)
            def _():
                pl.semaphore_signal(barrier, inc=1, device_id=peer, device_id_type=mesh_id)
            greeted = greeted + able.astype(jnp.int32)
    pl.semaphore_wait(barrier, greeted)

    if n_col > 2:
        for way in range(2):
            @pl.when(col == n_col - 1 if way == 0 else col == 0)
            def _():
                target_copy(way).start()
    for t in range(min(AHEAD, pieces)):
        send_own(t)
    for copy in tables:
        copy.wait()
    lag = max(n_col - 2, half_way - 1, 0)
    for step in range(pieces + lag):
        for dist in range(1, max(far, half_way) + 1):
            t = step - (dist - 1)
            if not 0 <= t < pieces:
                continue
            for way in range(2):
                if dist <= far:
                    @pl.when(receives(way, dist))
                    def _():
                        line_copy(way, dist, t).wait_recv()
                    if dist + 1 <= far:
                        @pl.when(can_send(way, dist + 1))
                        def _():
                            line_copy(way, dist + 1, t).start()
                if n_row > 1 and dist <= half_way:
                    ring_copy(way, dist, t).wait_recv()
                    if dist + 1 <= half_way:
                        ring_copy(way, dist + 1, t).start()
        if AHEAD + step < pieces:
            send_own(AHEAD + step)
        if n_col > 2:
            if 0 <= step - (n_col - 3) < pieces:
                fill_slots(step - (n_col - 3))
            if 0 <= step - (n_col - 2) < pieces:
                await_slots(step - (n_col - 2))
        if 0 <= step - lag < pieces:
            accumulate(step - lag)

    def row_basis(t, p):
        return jnp.concatenate([lbuf[t][left_index(tgt, p, k, True), 0] for k in range(KD)], axis=0)

    def twin_copy(which, src, dst):
        return pltpu.make_async_remote_copy(
            src_ref=src, dst_ref=dst, send_sem=xs_sem.at[which], recv_sem=xr_sem.at[which], device_id=twin, device_id_type=mesh_id)

    z_copies = [twin_copy(p, zpart.at[p], zrecv.at[p]) for p in range(tiles)]
    for p in range(tiles):
        folded = jnp.concatenate([mul_t(acc_v[p, k], acc_m[p, k]) for k in range(KD)], axis=1)
        for t in range(pieces):
            zpart[p, :, t * piece : (t + 1) * piece] = mul(folded, row_basis(t, p))
        z_copies[p].start()
    grams, sides = [], []
    for p in range(tiles):
        z_copies[p].wait()
        zpart[p] = zpart[p] + zrecv[p]
        gram, side = None, None
        for t in range(pieces):
            z = zpart[p, :, t * piece : (t + 1) * piece]
            g, s = mul_t(z, z), mul_t(z, row_basis(t, p))
            gram, side = (g, s) if t == 0 else (gram + g, side + s)
        grams.append(gram)
        sides.append(side)
    inverses = inverse_factor(grams)
    for p in range(tiles):
        linv[p] = inverses[p]
        turned = mul(inverses[p], sides[p])
        inner[p] = jnp.concatenate(
            [mul(turned[:, k * rank : (k + 1) * rank], acc_m[p, k]) for k in range(KD)], axis=1)

    owned = tiles // n_depth
    root = math.sqrt(width)

    def project(p, t):
        cols = jnp.concatenate([ubuf[t][up_index(p, k), 1] for k in range(KD)], axis=0)
        return mul(inner[p], cols)

    h_copy = twin_copy(tiles, hpart, hrecv)
    for i in range(owned):
        for t in range(pieces):
            hpart[i, :, t * piece : (t + 1) * piece] = project(other * owned + i, t)
    h_copy.start()
    for i in range(owned):
        p = dep * owned + i
        for t in range(pieces):
            cut = slice(t * piece, (t + 1) * piece)
            out_b[i, :, cut] = mul(linv[p], zpart[p, :, cut]) * root
            out_w[i, :, cut] = project(p, t)
    h_copy.wait()
    for i in range(owned):
        out_w[i] = (out_w[i] + hrecv[i]) / root

    if n_col > 2:
        for way in range(2):
            @pl.when(col == n_col - 1 if way == 0 else col == 0)
            def _():
                target_copy(way).wait_send()
    for t in range(pieces):
        for way in range(2):
            for dist in range(1, far + 1):
                @pl.when(can_send(way, dist))
                def _():
                    line_copy(way, dist, t).wait_send()
            if n_col > 2:
                @pl.when(col == n_col - 2 if way == 0 else col == 1)
                def _():
                    slot_copy(way, t).wait_send()
            if n_row > 1:
                for dist in range(1, half_way + 1):
                    ring_copy(way, dist, t).wait_send()


def solution(mesh):
    sizes = tuple(mesh.shape[a] for a in ("row", "col", "depth"))
    n_row, n_col, n_depth = sizes

    def shards(left_store, left_home, up_store, up_home, targets, sketch):
        lheld, _, rank, width = left_store.shape[2:]
        uheld = up_store.shape[2]
        tiles = targets.shape[2]
        slots = tiles * KD
        owned = tiles // n_depth
        piece = width // PIECES
        f32 = jnp.float32
        dma = pltpu.SemaphoreType.DMA
        far, half_way = max(n_col - 2, 1), max(n_row // 2, 1)
        out = jax.ShapeDtypeStruct((owned, rank, width), f32)
        vmem, smem = pl.BlockSpec(memory_space=pltpu.VMEM), pltpu.SMEM
        anywhere = pl.BlockSpec(memory_space=pl.ANY)
        basis, weights = pl.pallas_call(
            functools.partial(kernel, sizes),
            out_shape=(out, out),
            in_specs=[anywhere] * 6,
            out_specs=(vmem, vmem),
            scratch_shapes=[pltpu.VMEM((n_col * lheld + slots, 2, rank, piece), f32)] * PIECES
            + [pltpu.VMEM((n_row * uheld, 2, rank, piece), f32)] * PIECES
            + [pltpu.VMEM((2, slots, 2, rank, piece), f32)] * PIECES
            + [
                pltpu.VMEM((tiles, KD, rank, rank), f32),
                pltpu.VMEM((tiles, KD, rank, rank), f32),
                pltpu.VMEM((tiles, rank, width), f32),
                pltpu.VMEM((tiles, rank, width), f32),
                pltpu.VMEM((owned, rank, width), f32),
                pltpu.VMEM((owned, rank, width), f32),
                pltpu.VMEM((tiles, rank, KD * rank), f32),
                pltpu.VMEM((tiles, rank, rank), f32),
                smem(targets.shape, jnp.int32),
                smem((2,) + targets.shape, jnp.int32),
                smem(left_home.shape, jnp.int32),
                smem(up_home.shape, jnp.int32),
                pltpu.VMEM(sketch.shape[2:], f32),
                dma((4,)),
                dma((2,)),
                dma((2,)),
                dma((2, PIECES)),
                dma((2, far, PIECES)),
                dma((2, far, PIECES)),
                dma((2, half_way, PIECES)),
                dma((2, half_way, PIECES)),
                dma((2, PIECES)),
                dma((2, PIECES)),
                dma((tiles + 1,)),
                dma((tiles + 1,)),
            ],
            compiler_params=pltpu.CompilerParams(
                collective_id=0, has_side_effects=True, vmem_limit_bytes=60 * 1024 * 1024),
        )(targets, left_home, up_home, left_store, up_store, sketch)
        return basis[None, None], weights[None, None]

    return jax.shard_map(
        shards,
        mesh=mesh,
        in_specs=(
            P("row", "depth", "col", None, None, None),
            P("row", "depth", None),
            P("col", "depth", "row", None, None, None),
            P("col", "depth", None),
            P("row", "col", None),
            P("row", "col", None, None, None),
        ),
        out_specs=(P("row", "col", "depth", None, None), P("row", "col", "depth", None, None)),
        check_vma=False,
    )
```

```python
import functools
import math

import jax
import jax.numpy as jnp
from jax import lax
from jax.experimental import pallas as pl
from jax.experimental.pallas import tpu as pltpu
from jax.sharding import PartitionSpec as P

KD = 2
RB = 8
CB = 8
PIECES = 8
AHEAD = 4
HIGH = lax.Precision.HIGHEST


def mul(a, b):
    return lax.dot_general(a, b, (((1,), (0,)), ((), ())), precision=HIGH, preferred_element_type=jnp.float32)


def mul_t(a, b):
    return lax.dot_general(a, b, (((1,), (1,)), ((), ())), precision=HIGH, preferred_element_type=jnp.float32)


def inverse_factor(grams):
    n = grams[0].shape[0]
    row = lax.broadcasted_iota(jnp.int32, (n, n), 0)
    col = lax.broadcasted_iota(jnp.int32, (n, n), 1)
    eye = (row == col).astype(jnp.float32)
    work = [[jnp.concatenate([g, eye], axis=1)[i : i + 8] for i in range(0, n, 8)] for g in grams]
    sub = lax.broadcasted_iota(jnp.int32, (8, 1), 0)
    for j in range(n - 1):
        top, inside = j // 8, j % 8
        for blocks in work:
            line = blocks[top][inside : inside + 1, :]
            line = line / line[:, j : j + 1]
            for b in range(top, n // 8):
                factor = blocks[b][:, j : j + 1]
                if b == top:
                    if inside == 7:
                        continue
                    factor = jnp.where(sub > inside, factor, 0.0)
                blocks[b] = blocks[b] - factor * line
    results = []
    for blocks in work:
        whole = jnp.concatenate(blocks, axis=0)
        pivots = jnp.sum(whole[:, :n] * eye, axis=1, keepdims=True)
        results.append(whole[:, n:] / jnp.sqrt(pivots))
    return results


def ring_maps(n):
    side = math.isqrt(n)
    if side * side != n:
        return (lambda r: r), (lambda q: q)

    def swap(r):
        y, x = r // side, r % side
        return y * side + jnp.where(y % 2 == 0, x, side - 1 - x)

    return swap, swap


def kernel(sizes, tgt_in, lhome_in, uhome_in, left_in, up_in, sketch_in, out_b, out_w, *scratch):
    n_row, n_col, n_depth = sizes
    pieces = PIECES
    units = 2 * pieces
    lbuf, scratch = scratch[:units], scratch[units:]
    pack, scratch = scratch[:units], scratch[units:]
    ubuf, scratch = scratch[:pieces], scratch[pieces:]
    (acc_m, acc_v, acc_g, acc_s, zpart, zrecv, hpart, hrecv, inner, linv,
     tgt, tgt_end, lhome, uhome, sketch, tab_sem, ts_sem, tr_sem, loc_sem, zs_sem, zr_sem, rs_sem, rr_sem, ks_sem, kr_sem, xs_sem, xr_sem) = scratch
    left, up = left_in.at[0, 0], up_in.at[0, 0]
    lheld, uheld = left.shape[0], up.shape[0]
    tiles, rank, width = sketch.shape
    piece = width // pieces
    slots = tiles * KD
    row, col, dep = lax.axis_index("row"), lax.axis_index("col"), lax.axis_index("depth")
    other = n_depth - 1 - dep
    to_ring, from_ring = ring_maps(n_row)
    spot = to_ring(row)
    half_way = n_row // 2

    def ring_row(offset):
        return from_ring((spot + offset + n_row) % n_row)

    right, left_of = (row, col + 1, dep), (row, col - 1, dep)
    after, before = (ring_row(1), col, dep), (ring_row(-1), col, dep)
    twin = (row, col, other)
    mesh_id = pl.DeviceIdType.MESH

    def local_line(u):
        factor = 1 if u < pieces else 0
        cut = pl.ds((u % pieces) * piece, piece)
        return pltpu.make_async_copy(left.at[:, factor, :, cut], lbuf[u].at[pl.ds(col * lheld, lheld)], loc_sem.at[u])

    def local_ring(t):
        cut = pl.ds(t * piece, piece)
        return pltpu.make_async_copy(up.at[:, :, :, cut], ubuf[t].at[pl.ds(row * uheld, uheld)], loc_sem.at[units + t])

    def line_copy(way, dist, t):
        source = col - (dist - 1) if way == 0 else col + (dist - 1)
        view = lbuf[t].at[pl.ds(source * lheld, lheld)]
        return pltpu.make_async_remote_copy(
            src_ref=view, dst_ref=view, send_sem=zs_sem.at[way, dist - 1, t], recv_sem=zr_sem.at[way, dist - 1, t],
            device_id=right if way == 0 else left_of, device_id_type=mesh_id)

    def slot_copy(way, t):
        return pltpu.make_async_remote_copy(
            src_ref=pack[t].at[way], dst_ref=lbuf[t].at[pl.ds(n_col * lheld, slots)], send_sem=ks_sem.at[way, t],
            recv_sem=kr_sem.at[way, t], device_id=right if way == 0 else left_of, device_id_type=mesh_id)

    def ring_copy(way, dist, t):
        source = ring_row(1 - dist if way == 0 else dist - 1)
        view = ubuf[t].at[pl.ds(source * uheld, uheld)]
        if n_row % 2 == 0 and dist == half_way:
            view = ubuf[t].at[pl.ds(source * uheld, uheld), way]
        return pltpu.make_async_remote_copy(
            src_ref=view, dst_ref=view, send_sem=rs_sem.at[way, dist - 1, t], recv_sem=rr_sem.at[way, dist - 1, t],
            device_id=after if way == 0 else before, device_id_type=mesh_id)

    def can_send(way, dist):
        if way == 0:
            end = col < n_col - 1 if dist == 1 else col < n_col - 2
            return jnp.logical_and(col - (dist - 1) >= 0, end)
        end = col > 0 if dist == 1 else col > 1
        return jnp.logical_and(col + (dist - 1) <= n_col - 1, end)

    def receives(way, dist):
        if way == 0:
            if dist == 1:
                return col >= 1
            return jnp.logical_and(col - dist >= 0, col < n_col - 1)
        if dist == 1:
            return col <= n_col - 2
        return jnp.logical_and(col + dist <= n_col - 1, col > 0)

    far = max(n_col - 2, 1) if n_col > 1 else 0

    def left_index(table, p, k, packed):
        pos = lhome[0, 0, (table[0, 0, p] // CB) * KD + k]
        if not packed or n_col < 3:
            return pos
        source = pos // lheld
        by_slot = jnp.logical_or(
            jnp.logical_and(col == 0, source >= 2), jnp.logical_and(col == n_col - 1, source <= n_col - 3))
        return jnp.where(by_slot, n_col * lheld + p * KD + k, pos)

    def up_index(p, k):
        return uhome[0, 0, (tgt[0, 0, p] % CB) * KD + k]

    def send_line(u):
        local_line(u).wait()
        for way in range(2):
            if n_col > 1:
                @pl.when(can_send(way, 1))
                def _():
                    line_copy(way, 1, u).start()

    def send_ring(t):
        local_ring(t).wait()
        for way in range(2):
            if n_row > 1:
                ring_copy(way, 1, t).start()

    def fill_slots(t):
        for way in range(2):
            turn = col == n_col - 2 if way == 0 else col == 1

            @pl.when(turn)
            def _():
                if t == 0:
                    target_copy(way).wait_recv()
                for p in range(tiles):
                    for k in range(KD):
                        pack[t][way, p * KD + k] = lbuf[t][left_index(tgt_end.at[way], p, k, False)]
                slot_copy(way, t).start()

    def await_slots(t):
        for way in range(2):
            @pl.when(col == n_col - 1 if way == 0 else col == 0)
            def _():
                slot_copy(way, t).wait_recv()

    def accumulate(t):
        for p in range(tiles):
            tests = sketch[p, :, t * piece : (t + 1) * piece]
            for k in range(KD):
                coef = lbuf[t][left_index(tgt, p, k, True)]
                pair = ubuf[t].at[up_index(p, k)]
                middle = mul_t(coef, pair[0])
                tested = mul_t(tests, pair[1])
                if t == 0:
                    acc_m[p, k] = middle
                    acc_v[p, k] = tested
                else:
                    acc_m[p, k] += middle
                    acc_v[p, k] += tested

    tables = [
        pltpu.make_async_copy(src, dst, tab_sem.at[i])
        for i, (src, dst) in enumerate(((tgt_in, tgt), (lhome_in, lhome), (uhome_in, uhome), (sketch_in.at[0, 0], sketch)))
    ]

    def target_copy(way):
        return pltpu.make_async_remote_copy(
            src_ref=tgt_in, dst_ref=tgt_end.at[way], send_sem=ts_sem.at[way], recv_sem=tr_sem.at[way],
            device_id=left_of if way == 0 else right, device_id_type=mesh_id)

    for u in range(units):
        local_line(u).start()
        if u < pieces:
            local_ring(u).start()
    for copy in tables:
        copy.start()

    barrier = pltpu.get_barrier_semaphore()
    peers = [twin] + ([after, before] if n_row > 1 else [])
    for peer in peers:
        pl.semaphore_signal(barrier, inc=1, device_id=peer, device_id_type=mesh_id)
    greeted = len(peers)
    if n_col > 1:
        for able, peer in ((col < n_col - 1, right), (col > 0, left_of)):
            @pl.when(able)
            def _():
                pl.semaphore_signal(barrier, inc=1, device_id=peer, device_id_type=mesh_id)
            greeted = greeted + able.astype(jnp.int32)
    pl.semaphore_wait(barrier, greeted)

    if n_col > 2:
        for way in range(2):
            @pl.when(col == n_col - 1 if way == 0 else col == 0)
            def _():
                target_copy(way).start()
    def row_basis(t, p):
        return jnp.concatenate([lbuf[pieces + t][left_index(tgt, p, k, True)] for k in range(KD)], axis=0)

    def twin_copy(which, src, dst):
        return pltpu.make_async_remote_copy(
            src_ref=src, dst_ref=dst, send_sem=xs_sem.at[which], recv_sem=xr_sem.at[which], device_id=twin, device_id_type=mesh_id)

    def z_copy(t):
        return twin_copy(t, zpart.at[t], zrecv.at[t])

    def fold():
        for p in range(tiles):
            inner[p] = jnp.concatenate([mul_t(acc_v[p, k], acc_m[p, k]) for k in range(KD)], axis=1)

    def sample(t):
        for p in range(tiles):
            zpart[t, p] = mul(inner[p], row_basis(t, p))
        z_copy(t).start()

    def gather_grams(t):
        z_copy(t).wait()
        for p in range(tiles):
            z = zpart[t, p] + zrecv[t, p]
            zpart[t, p] = z
            g, s = mul_t(z, z), mul_t(z, row_basis(t, p))
            if t == 0:
                acc_g[p] = g
                acc_s[p] = s
            else:
                acc_g[p] += g
                acc_s[p] += s

    ring_at = [(3 * t) // 2 for t in range(pieces)]
    for u in range(min(AHEAD, units)):
        send_line(u)
        for t in range(pieces):
            if ring_at[t] == u:
                send_ring(t)
    for copy in tables:
        copy.wait()
    line_lag, ring_lag = max(n_col - 2, 0), max(half_way - 1, 0)
    lag = max(line_lag, ring_lag)
    sampled = 0
    for step in range(units + lag):
        for dist in range(1, max(far, half_way) + 1):
            u = step - (dist - 1)
            for way in range(2):
                if dist <= far and 0 <= u < units:
                    @pl.when(receives(way, dist))
                    def _():
                        line_copy(way, dist, u).wait_recv()
                    if dist + 1 <= far:
                        @pl.when(can_send(way, dist + 1))
                        def _():
                            line_copy(way, dist + 1, u).start()
                if n_row > 1 and dist <= half_way and u in ring_at:
                    t = ring_at.index(u)
                    ring_copy(way, dist, t).wait_recv()
                    if dist + 1 <= half_way:
                        ring_copy(way, dist + 1, t).start()
        if AHEAD + step < units:
            send_line(AHEAD + step)
            if AHEAD + step in ring_at:
                send_ring(ring_at.index(AHEAD + step))
        if n_col > 2:
            if 0 <= step - (n_col - 3) < units:
                fill_slots(step - (n_col - 3))
            if 0 <= step - (n_col - 2) < units:
                await_slots(step - (n_col - 2))
        u = step - lag
        if u in ring_at:
            accumulate(ring_at.index(u))
        if u == ring_at[-1]:
            fold()
        elif u > ring_at[-1]:
            ready = u - pieces + 1
            for t in range(sampled, ready):
                sample(t)
                if t > 0:
                    gather_grams(t - 1)
            sampled = ready
    gather_grams(pieces - 1)
    grams = [acc_g[p] for p in range(tiles)]
    sides = [acc_s[p] for p in range(tiles)]
    inverses = inverse_factor(grams)
    for p in range(tiles):
        linv[p] = inverses[p]
        turned = mul(inverses[p], sides[p])
        inner[p] = jnp.concatenate(
            [mul(turned[:, k * rank : (k + 1) * rank], acc_m[p, k]) for k in range(KD)], axis=1)

    owned = tiles // n_depth
    root = math.sqrt(width)

    def project(p, t):
        cols = jnp.concatenate([ubuf[t][up_index(p, k), 1] for k in range(KD)], axis=0)
        return mul(inner[p], cols)

    h_copy = twin_copy(pieces, hpart, hrecv)
    for i in range(owned):
        for t in range(pieces):
            hpart[i, :, t * piece : (t + 1) * piece] = project(other * owned + i, t)
    h_copy.start()
    for i in range(owned):
        p = dep * owned + i
        for t in range(pieces):
            cut = slice(t * piece, (t + 1) * piece)
            out_b[i, :, cut] = mul(linv[p], zpart[t, p]) * root
            out_w[i, :, cut] = project(p, t)
    h_copy.wait()
    for i in range(owned):
        out_w[i] = (out_w[i] + hrecv[i]) / root

    if n_col > 2:
        for way in range(2):
            @pl.when(col == n_col - 1 if way == 0 else col == 0)
            def _():
                target_copy(way).wait_send()
    for t in range(units):
        for way in range(2):
            for dist in range(1, far + 1):
                @pl.when(can_send(way, dist))
                def _():
                    line_copy(way, dist, t).wait_send()
            if n_col > 2:
                @pl.when(col == n_col - 2 if way == 0 else col == 1)
                def _():
                    slot_copy(way, t).wait_send()
            if n_row > 1 and t < pieces:
                for dist in range(1, half_way + 1):
                    ring_copy(way, dist, t).wait_send()


def solution(mesh):
    sizes = tuple(mesh.shape[a] for a in ("row", "col", "depth"))
    n_row, n_col, n_depth = sizes

    def shards(left_store, left_home, up_store, up_home, targets, sketch):
        lheld, _, rank, width = left_store.shape[2:]
        uheld = up_store.shape[2]
        tiles = targets.shape[2]
        slots = tiles * KD
        owned = tiles // n_depth
        piece, units = width // PIECES, 2 * PIECES
        f32 = jnp.float32
        dma = pltpu.SemaphoreType.DMA
        far, half_way = max(n_col - 2, 1), max(n_row // 2, 1)
        out = jax.ShapeDtypeStruct((owned, rank, width), f32)
        vmem, smem = pl.BlockSpec(memory_space=pltpu.VMEM), pltpu.SMEM
        anywhere = pl.BlockSpec(memory_space=pl.ANY)
        basis, weights = pl.pallas_call(
            functools.partial(kernel, sizes),
            out_shape=(out, out),
            in_specs=[anywhere] * 6,
            out_specs=(vmem, vmem),
            scratch_shapes=[pltpu.VMEM((n_col * lheld + slots, rank, piece), f32)] * units
            + [pltpu.VMEM((2, slots, rank, piece), f32)] * units
            + [pltpu.VMEM((n_row * uheld, 2, rank, piece), f32)] * PIECES
            + [
                pltpu.VMEM((tiles, KD, rank, rank), f32),
                pltpu.VMEM((tiles, KD, rank, rank), f32),
                pltpu.VMEM((tiles, rank, rank), f32),
                pltpu.VMEM((tiles, rank, KD * rank), f32),
                pltpu.VMEM((PIECES, tiles, rank, piece), f32),
                pltpu.VMEM((PIECES, tiles, rank, piece), f32),
                pltpu.VMEM((owned, rank, width), f32),
                pltpu.VMEM((owned, rank, width), f32),
                pltpu.VMEM((tiles, rank, KD * rank), f32),
                pltpu.VMEM((tiles, rank, rank), f32),
                smem(targets.shape, jnp.int32),
                smem((2,) + targets.shape, jnp.int32),
                smem(left_home.shape, jnp.int32),
                smem(up_home.shape, jnp.int32),
                pltpu.VMEM(sketch.shape[2:], f32),
                dma((4,)),
                dma((2,)),
                dma((2,)),
                dma((units + PIECES,)),
                dma((2, far, units)),
                dma((2, far, units)),
                dma((2, half_way, PIECES)),
                dma((2, half_way, PIECES)),
                dma((2, units)),
                dma((2, units)),
                dma((PIECES + 1,)),
                dma((PIECES + 1,)),
            ],
            compiler_params=pltpu.CompilerParams(
                collective_id=0, has_side_effects=True, vmem_limit_bytes=60 * 1024 * 1024),
        )(targets, left_home, up_home, left_store, up_store, sketch)
        return basis[None, None], weights[None, None]

    return jax.shard_map(
        shards,
        mesh=mesh,
        in_specs=(
            P("row", "depth", "col", None, None, None),
            P("row", "depth", None),
            P("col", "depth", "row", None, None, None),
            P("col", "depth", None),
            P("row", "col", None),
            P("row", "col", None, None, None),
        ),
        out_specs=(P("row", "col", "depth", None, None), P("row", "col", "depth", None, None)),
        check_vma=False,
    )
```

```python
import functools
import math

import jax
import jax.numpy as jnp
from jax import lax
from jax.experimental import pallas as pl
from jax.experimental.pallas import tpu as pltpu
from jax.sharding import PartitionSpec as P

KD = 2
RB = 8
CB = 8
PIECES = 8
AHEAD = 2
HIGH = lax.Precision.HIGHEST


def mul(a, b):
    return lax.dot_general(a, b, (((1,), (0,)), ((), ())), precision=HIGH, preferred_element_type=jnp.float32)


def mul_t(a, b):
    return lax.dot_general(a, b, (((1,), (1,)), ((), ())), precision=HIGH, preferred_element_type=jnp.float32)


def inverse_factor(grams):
    n = grams[0].shape[0]
    row = lax.broadcasted_iota(jnp.int32, (n, n), 0)
    col = lax.broadcasted_iota(jnp.int32, (n, n), 1)
    eye = (row == col).astype(jnp.float32)
    work = [[jnp.concatenate([g, eye], axis=1)[i : i + 8] for i in range(0, n, 8)] for g in grams]
    sub = lax.broadcasted_iota(jnp.int32, (8, 1), 0)
    for j in range(n - 1):
        top, inside = j // 8, j % 8
        for blocks in work:
            line = blocks[top][inside : inside + 1, :]
            line = line / line[:, j : j + 1]
            for b in range(top, n // 8):
                factor = blocks[b][:, j : j + 1]
                if b == top:
                    if inside == 7:
                        continue
                    factor = jnp.where(sub > inside, factor, 0.0)
                blocks[b] = blocks[b] - factor * line
    results = []
    for blocks in work:
        whole = jnp.concatenate(blocks, axis=0)
        pivots = jnp.sum(whole[:, :n] * eye, axis=1, keepdims=True)
        results.append(whole[:, n:] / jnp.sqrt(pivots))
    return results


def ring_maps(n):
    side = math.isqrt(n)
    if side * side != n:
        return (lambda r: r), (lambda q: q)

    def swap(r):
        y, x = r // side, r % side
        return y * side + jnp.where(y % 2 == 0, x, side - 1 - x)

    return swap, swap


def kernel(sizes, tgt_in, lhome_in, uhome_in, left_in, up_in, sketch_in, out_b, out_w, *scratch):
    n_row, n_col, n_depth = sizes
    pieces = PIECES
    units = 2 * pieces
    lbuf, scratch = scratch[:units], scratch[units:]
    pack, scratch = scratch[:units], scratch[units:]
    ubuf, scratch = scratch[:pieces], scratch[pieces:]
    (acc_m, acc_v, acc_g, acc_s, zpart, zrecv, hpart, hrecv, inner, linv,
     tgt, tgt_end, lhome, uhome, sketch, tab_sem, ts_sem, tr_sem, loc_sem, zs_sem, zr_sem, rs_sem, rr_sem, ks_sem, kr_sem, xs_sem, xr_sem) = scratch
    left, up = left_in.at[0, 0], up_in.at[0, 0]
    lheld, uheld = left.shape[0], up.shape[0]
    tiles, rank, width = sketch.shape
    piece = width // pieces
    slots = tiles * KD
    row, col, dep = lax.axis_index("row"), lax.axis_index("col"), lax.axis_index("depth")
    other = n_depth - 1 - dep
    to_ring, from_ring = ring_maps(n_row)
    spot = to_ring(row)
    half_way = n_row // 2

    def ring_row(offset):
        return from_ring((spot + offset + n_row) % n_row)

    right, left_of = (row, col + 1, dep), (row, col - 1, dep)
    after, before = (ring_row(1), col, dep), (ring_row(-1), col, dep)
    twin = (row, col, other)
    mesh_id = pl.DeviceIdType.MESH

    def local_line(u):
        factor = 1 if u < pieces else 0
        cut = pl.ds((u % pieces) * piece, piece)
        return pltpu.make_async_copy(left.at[:, factor, :, cut], lbuf[u].at[pl.ds(col * lheld, lheld)], loc_sem.at[u])

    def local_ring(t):
        cut = pl.ds(t * piece, piece)
        return pltpu.make_async_copy(up.at[:, :, :, cut], ubuf[t].at[pl.ds(row * uheld, uheld)], loc_sem.at[units + t])

    def line_copy(way, dist, t):
        source = col - (dist - 1) if way == 0 else col + (dist - 1)
        view = lbuf[t].at[pl.ds(source * lheld, lheld)]
        return pltpu.make_async_remote_copy(
            src_ref=view, dst_ref=view, send_sem=zs_sem.at[way, dist - 1, t], recv_sem=zr_sem.at[way, dist - 1, t],
            device_id=right if way == 0 else left_of, device_id_type=mesh_id)

    def slot_copy(way, t):
        return pltpu.make_async_remote_copy(
            src_ref=pack[t].at[way], dst_ref=lbuf[t].at[pl.ds(n_col * lheld, slots)], send_sem=ks_sem.at[way, t],
            recv_sem=kr_sem.at[way, t], device_id=right if way == 0 else left_of, device_id_type=mesh_id)

    def ring_copy(way, dist, t):
        source = ring_row(1 - dist if way == 0 else dist - 1)
        view = ubuf[t].at[pl.ds(source * uheld, uheld)]
        if n_row % 2 == 0 and dist == half_way:
            view = ubuf[t].at[pl.ds(source * uheld, uheld), way]
        return pltpu.make_async_remote_copy(
            src_ref=view, dst_ref=view, send_sem=rs_sem.at[way, dist - 1, t], recv_sem=rr_sem.at[way, dist - 1, t],
            device_id=after if way == 0 else before, device_id_type=mesh_id)

    def can_send(way, dist):
        if way == 0:
            end = col < n_col - 1 if dist == 1 else col < n_col - 2
            return jnp.logical_and(col - (dist - 1) >= 0, end)
        end = col > 0 if dist == 1 else col > 1
        return jnp.logical_and(col + (dist - 1) <= n_col - 1, end)

    def receives(way, dist):
        if way == 0:
            if dist == 1:
                return col >= 1
            return jnp.logical_and(col - dist >= 0, col < n_col - 1)
        if dist == 1:
            return col <= n_col - 2
        return jnp.logical_and(col + dist <= n_col - 1, col > 0)

    far = max(n_col - 2, 1) if n_col > 1 else 0

    def left_index(table, p, k, packed):
        pos = lhome[0, 0, (table[0, 0, p] // CB) * KD + k]
        if not packed or n_col < 3:
            return pos
        source = pos // lheld
        by_slot = jnp.logical_or(
            jnp.logical_and(col == 0, source >= 2), jnp.logical_and(col == n_col - 1, source <= n_col - 3))
        return jnp.where(by_slot, n_col * lheld + p * KD + k, pos)

    def up_index(p, k):
        return uhome[0, 0, (tgt[0, 0, p] % CB) * KD + k]

    def send_line(u):
        local_line(u).wait()
        for way in range(2):
            if n_col > 1:
                @pl.when(can_send(way, 1))
                def _():
                    line_copy(way, 1, u).start()

    def send_ring(t):
        local_ring(t).wait()
        for way in range(2):
            if n_row > 1:
                ring_copy(way, 1, t).start()

    def fill_slots(t):
        for way in range(2):
            turn = col == n_col - 2 if way == 0 else col == 1

            @pl.when(turn)
            def _():
                if t == 0:
                    target_copy(way).wait_recv()
                for p in range(tiles):
                    for k in range(KD):
                        pack[t][way, p * KD + k] = lbuf[t][left_index(tgt_end.at[way], p, k, False)]
                slot_copy(way, t).start()

    def await_slots(t):
        for way in range(2):
            @pl.when(col == n_col - 1 if way == 0 else col == 0)
            def _():
                slot_copy(way, t).wait_recv()

    def accumulate(t):
        for p in range(tiles):
            tests = sketch[p, :, t * piece : (t + 1) * piece]
            for k in range(KD):
                coef = lbuf[t][left_index(tgt, p, k, True)]
                pair = ubuf[t].at[up_index(p, k)]
                middle = mul_t(coef, pair[0])
                tested = mul_t(tests, pair[1])
                if t == 0:
                    acc_m[p, k] = middle
                    acc_v[p, k] = tested
                else:
                    acc_m[p, k] += middle
                    acc_v[p, k] += tested

    tables = [
        pltpu.make_async_copy(src, dst, tab_sem.at[i])
        for i, (src, dst) in enumerate(((tgt_in, tgt), (lhome_in, lhome), (uhome_in, uhome), (sketch_in.at[0, 0], sketch)))
    ]

    def target_copy(way):
        return pltpu.make_async_remote_copy(
            src_ref=tgt_in, dst_ref=tgt_end.at[way], send_sem=ts_sem.at[way], recv_sem=tr_sem.at[way],
            device_id=left_of if way == 0 else right, device_id_type=mesh_id)

    for u in range(units):
        local_line(u).start()
        if u < pieces:
            local_ring(u).start()
    for copy in tables:
        copy.start()

    barrier = pltpu.get_barrier_semaphore()
    peers = [twin] + ([after, before] if n_row > 1 else [])
    for peer in peers:
        pl.semaphore_signal(barrier, inc=1, device_id=peer, device_id_type=mesh_id)
    greeted = len(peers)
    if n_col > 1:
        for able, peer in ((col < n_col - 1, right), (col > 0, left_of)):
            @pl.when(able)
            def _():
                pl.semaphore_signal(barrier, inc=1, device_id=peer, device_id_type=mesh_id)
            greeted = greeted + able.astype(jnp.int32)
    pl.semaphore_wait(barrier, greeted)

    if n_col > 2:
        for way in range(2):
            @pl.when(col == n_col - 1 if way == 0 else col == 0)
            def _():
                target_copy(way).start()
    def row_basis(t, p):
        return jnp.concatenate([lbuf[pieces + t][left_index(tgt, p, k, True)] for k in range(KD)], axis=0)

    def twin_copy(which, src, dst):
        return pltpu.make_async_remote_copy(
            src_ref=src, dst_ref=dst, send_sem=xs_sem.at[which], recv_sem=xr_sem.at[which], device_id=twin, device_id_type=mesh_id)

    def z_copy(t):
        return twin_copy(t, zpart.at[t], zrecv.at[t])

    def fold():
        for p in range(tiles):
            inner[p] = jnp.concatenate([mul_t(acc_v[p, k], acc_m[p, k]) for k in range(KD)], axis=1)

    def sample(t):
        for p in range(tiles):
            zpart[t, p] = mul(inner[p], row_basis(t, p))
        z_copy(t).start()

    def gather_grams(t):
        z_copy(t).wait()
        for p in range(tiles):
            z = zpart[t, p] + zrecv[t, p]
            zpart[t, p] = z
            g, s = mul_t(z, z), mul_t(z, row_basis(t, p))
            if t == 0:
                acc_g[p] = g
                acc_s[p] = s
            else:
                acc_g[p] += g
                acc_s[p] += s

    ring_at = [(3 * t) // 2 for t in range(pieces)]
    for u in range(min(AHEAD, units)):
        send_line(u)
        for t in range(pieces):
            if ring_at[t] == u:
                send_ring(t)
    for copy in tables:
        copy.wait()
    line_lag, ring_lag = max(n_col - 2, 0), max(half_way - 1, 0)
    lag = max(line_lag, ring_lag)
    sampled = 0
    for step in range(units + lag):
        for dist in range(1, max(far, half_way) + 1):
            u = step - (dist - 1)
            for way in range(2):
                if dist <= far and 0 <= u < units:
                    @pl.when(receives(way, dist))
                    def _():
                        line_copy(way, dist, u).wait_recv()
                    if dist + 1 <= far:
                        @pl.when(can_send(way, dist + 1))
                        def _():
                            line_copy(way, dist + 1, u).start()
                if n_row > 1 and dist <= half_way and u in ring_at:
                    t = ring_at.index(u)
                    ring_copy(way, dist, t).wait_recv()
                    if dist + 1 <= half_way:
                        ring_copy(way, dist + 1, t).start()
        if AHEAD + step < units:
            send_line(AHEAD + step)
            if AHEAD + step in ring_at:
                send_ring(ring_at.index(AHEAD + step))
        if n_col > 2:
            if 0 <= step - (n_col - 3) < units:
                fill_slots(step - (n_col - 3))
            if 0 <= step - (n_col - 2) < units:
                await_slots(step - (n_col - 2))
        u = step - lag
        if u in ring_at:
            accumulate(ring_at.index(u))
        if u == ring_at[-1]:
            fold()
        elif u > ring_at[-1]:
            ready = u - pieces + 1
            for t in range(sampled, ready):
                sample(t)
                if t > 0:
                    gather_grams(t - 1)
            sampled = ready
    gather_grams(pieces - 1)
    grams = [acc_g[p] for p in range(tiles)]
    sides = [acc_s[p] for p in range(tiles)]
    inverses = inverse_factor(grams)
    for p in range(tiles):
        linv[p] = inverses[p]
        turned = mul(inverses[p], sides[p])
        inner[p] = jnp.concatenate(
            [mul(turned[:, k * rank : (k + 1) * rank], acc_m[p, k]) for k in range(KD)], axis=1)

    owned = tiles // n_depth
    root = math.sqrt(width)

    def project(p, t):
        cols = jnp.concatenate([ubuf[t][up_index(p, k), 1] for k in range(KD)], axis=0)
        return mul(inner[p], cols)

    h_copy = twin_copy(pieces, hpart, hrecv)
    for i in range(owned):
        for t in range(pieces):
            hpart[i, :, t * piece : (t + 1) * piece] = project(other * owned + i, t)
    h_copy.start()
    for i in range(owned):
        p = dep * owned + i
        for t in range(pieces):
            cut = slice(t * piece, (t + 1) * piece)
            out_b[i, :, cut] = mul(linv[p], zpart[t, p]) * root
            out_w[i, :, cut] = project(p, t)
    h_copy.wait()
    for i in range(owned):
        out_w[i] = (out_w[i] + hrecv[i]) / root

    if n_col > 2:
        for way in range(2):
            @pl.when(col == n_col - 1 if way == 0 else col == 0)
            def _():
                target_copy(way).wait_send()
    for t in range(units):
        for way in range(2):
            for dist in range(1, far + 1):
                @pl.when(can_send(way, dist))
                def _():
                    line_copy(way, dist, t).wait_send()
            if n_col > 2:
                @pl.when(col == n_col - 2 if way == 0 else col == 1)
                def _():
                    slot_copy(way, t).wait_send()
            if n_row > 1 and t < pieces:
                for dist in range(1, half_way + 1):
                    ring_copy(way, dist, t).wait_send()


def solution(mesh):
    sizes = tuple(mesh.shape[a] for a in ("row", "col", "depth"))
    n_row, n_col, n_depth = sizes

    def shards(left_store, left_home, up_store, up_home, targets, sketch):
        lheld, _, rank, width = left_store.shape[2:]
        uheld = up_store.shape[2]
        tiles = targets.shape[2]
        slots = tiles * KD
        owned = tiles // n_depth
        piece, units = width // PIECES, 2 * PIECES
        f32 = jnp.float32
        dma = pltpu.SemaphoreType.DMA
        far, half_way = max(n_col - 2, 1), max(n_row // 2, 1)
        out = jax.ShapeDtypeStruct((owned, rank, width), f32)
        vmem, smem = pl.BlockSpec(memory_space=pltpu.VMEM), pltpu.SMEM
        anywhere = pl.BlockSpec(memory_space=pl.ANY)
        basis, weights = pl.pallas_call(
            functools.partial(kernel, sizes),
            out_shape=(out, out),
            in_specs=[anywhere] * 6,
            out_specs=(vmem, vmem),
            scratch_shapes=[pltpu.VMEM((n_col * lheld + slots, rank, piece), f32)] * units
            + [pltpu.VMEM((2, slots, rank, piece), f32)] * units
            + [pltpu.VMEM((n_row * uheld, 2, rank, piece), f32)] * PIECES
            + [
                pltpu.VMEM((tiles, KD, rank, rank), f32),
                pltpu.VMEM((tiles, KD, rank, rank), f32),
                pltpu.VMEM((tiles, rank, rank), f32),
                pltpu.VMEM((tiles, rank, KD * rank), f32),
                pltpu.VMEM((PIECES, tiles, rank, piece), f32),
                pltpu.VMEM((PIECES, tiles, rank, piece), f32),
                pltpu.VMEM((owned, rank, width), f32),
                pltpu.VMEM((owned, rank, width), f32),
                pltpu.VMEM((tiles, rank, KD * rank), f32),
                pltpu.VMEM((tiles, rank, rank), f32),
                smem(targets.shape, jnp.int32),
                smem((2,) + targets.shape, jnp.int32),
                smem(left_home.shape, jnp.int32),
                smem(up_home.shape, jnp.int32),
                pltpu.VMEM(sketch.shape[2:], f32),
                dma((4,)),
                dma((2,)),
                dma((2,)),
                dma((units + PIECES,)),
                dma((2, far, units)),
                dma((2, far, units)),
                dma((2, half_way, PIECES)),
                dma((2, half_way, PIECES)),
                dma((2, units)),
                dma((2, units)),
                dma((PIECES + 1,)),
                dma((PIECES + 1,)),
            ],
            compiler_params=pltpu.CompilerParams(
                collective_id=0, has_side_effects=True, vmem_limit_bytes=60 * 1024 * 1024),
        )(targets, left_home, up_home, left_store, up_store, sketch)
        return basis[None, None], weights[None, None]

    return jax.shard_map(
        shards,
        mesh=mesh,
        in_specs=(
            P("row", "depth", "col", None, None, None),
            P("row", "depth", None),
            P("col", "depth", "row", None, None, None),
            P("col", "depth", None),
            P("row", "col", None),
            P("row", "col", None, None, None),
        ),
        out_specs=(P("row", "col", "depth", None, None), P("row", "col", "depth", None, None)),
        check_vma=False,
    )
```
